32 devices in a mesh: layer: 2 (over x), tok: 16 (over z, y, core).
Axes of the slice: x: 2, y: 2, z: 4, core: 2. Of those that a mesh axis runs over, the one named last changes fastest.
Arguments:
- tokens: bfloat16 [4096, 7168], P(('layer', 'tok')), parts along dimension 0, may hold values from -22 to 22
- out_grads: bfloat16 [4096, 1024], P(('layer', 'tok')), parts along dimension 0, may hold values from -22 to 22
- routing: int32 [4096, 1], P(('layer', 'tok')), parts along dimension 0, may hold values from 0 to 3; in each aligned block of 128 rows (0 to 127, 128 to 255, ...) at most 48 rows name the same one
- weights: bfloat16 [8, 7168, 1024], P('layer', 'tok'), parts along dimension 0, may hold values from -6 to 6
Outputs:
- fisher: float32 [8, 7168, 1024], P('layer', 'tok'), parts along dimension 0
- merged: bfloat16 [14336, 1024], P(('layer', 'tok')), parts along dimension 0
The draws below stay inside these ranges and needn't reach their ends.
There are 2 independent parts, one for each index of `layer`. The reference program is written for one: setup_inputs(seed, part) draws one part's arguments, and reference() takes and returns one part's arrays. A program takes and returns all parts, laid end to end along the dimension named above; each array names one. Nothing has to cross between parts.
Inputs may be any that keep to these rules, and one draw needn't show every extreme that they name: `routing`: each row names one expert; of the rows of one device at most 48 name the same expert, and that count is reached on some device.
All inputs are finite; a program needn't handle non-finite values.
Results may differ from the reference program's by a relative error of at most 0.0004.
Values may be sent and summed in bfloat16 or wider, within the bound.
No kernel may reach another device: no remote copies, remote signals or barrier semaphores. Data moves between devices by JAX's collectives and lax.ppermute only.
A program may use at most 128 MiB of HBM per device.

```python
import math
import jax
import jax.numpy as jnp
import numpy as np
from jax import lax

D = 7168
F = 1024
E = 4
TOK_DEV = 128
CAP = 48
TOKENS = 2048
N_TOK = 16


def draw_tokens(key, part):
    key = jax.random.fold_in(key, 11)
    spread_key, noise_key = jax.random.split(key)
    position = jnp.arange(D, dtype=jnp.float32) / D
    spread = jnp.exp(jax.random.uniform(spread_key, (D,), jnp.float32, 0.0, 0.5 * math.log(10.0)))
    rising = jnp.exp(0.5 * math.log(3.0) * position)
    noise = jax.random.truncated_normal(noise_key, -4.0, 4.0, (TOKENS, D), jnp.float32)
    return (noise * (rising * spread)[None, :]).astype(jnp.bfloat16)


def draw_out_grads(key, part):
    key = jax.random.fold_in(key, 23)
    spread_key, noise_key = jax.random.split(key, 2)
    position = jnp.arange(TOKENS, dtype=jnp.float32) / TOKENS
    spread = jnp.exp(jax.random.uniform(spread_key, (TOKENS,), jnp.float32, 0.0, 0.5 * math.log(10.0)))
    rising = jnp.exp(0.5 * math.log(3.0) * position)
    noise = jax.random.truncated_normal(noise_key, -4.0, 4.0, (TOKENS, F), jnp.float32)
    return (noise * (rising * spread)[:, None]).astype(jnp.bfloat16)


def block_scale(rng, extent, shards, smallest, largest):
    factor_of = 1.0
    for dim, shards_of in shards:
        heights = jax.random.uniform(jax.random.fold_in(jax.random.fold_in(rng, 6), dim), (shards_of,), jnp.float32, smallest / len(shards), largest / len(shards))
        factor_of = factor_of * jnp.repeat(jnp.exp(heights), extent[dim] // shards_of).reshape((-1,) + (1,) * (len(extent) - 1 - dim))
    return factor_of


def assign_block(key, own, number, rows, count, top, reach, skew):
    order = jax.random.permutation(key, count)
    heavy_load, usual = portions_of(count, rows * top, reach, skew, True), portions_of(count, rows * top, reach, skew, False)
    places = jnp.arange(count)

    def named(lengths, rotation):
        used = int((lengths > 0).sum())
        fixed = max(1, used // 4)
        passed = fixed + (places - fixed + rotation * (used - fixed)) % max(1, count - fixed)
        return jnp.zeros((count,), jnp.int32).at[order[jnp.where(places < fixed, places, passed)]].set(jnp.asarray(lengths, jnp.int32))

    lengths = jnp.where(number % 4 == 0, named(heavy_load, number // 4), named(usual, number - number // 4 - 1))
    mixed = jax.random.permutation(jax.random.fold_in(own, 3), count)
    giver, sink = mixed[0:count // 2 * 2:2], mixed[1:count // 2 * 2:2]
    margin = jnp.minimum(lengths[giver] - 1, reach - lengths[sink]) // 2
    margin = jnp.where((giver == order[0]) | (sink == order[0]) | (lengths[sink] == 0), 0, jnp.maximum(margin, 0))
    passed = jax.random.randint(jax.random.fold_in(own, 4), (count // 2,), 0, 1 << 20) % (margin + 1)
    lengths = lengths.at[giver].add(-passed).at[sink].add(passed)
    items = jnp.searchsorted(jnp.cumsum(lengths), jnp.arange(rows * top), side="right").astype(jnp.int32)
    listing = items.reshape(top, rows).T
    listing = listing[jax.random.permutation(jax.random.fold_in(own, 1), rows)]
    rotation = jax.random.randint(jax.random.fold_in(own, 2), (rows, 1), 0, top)
    return jnp.take_along_axis(listing, (jnp.arange(top)[None, :] + rotation) % top, axis=1)


def portions_of(amount, total, most, lean, full):
    portions = [(1 << 20) // math.isqrt(rank ** lean) + 1 for rank in range(1, amount + 1)]
    largest = most if full else min(most, max(-(-total // amount), total * portions[0] // sum(portions)))
    least = 1 if total - largest >= amount - 1 else 0
    given, rest = [largest] + [least] * (amount - 1), total - largest - least * (amount - 1)
    while rest > 0:
        candidates = [i for i in range(1, amount) if given[i] < largest] or [i for i in range(1, amount) if given[i] < most]
        pool, remaining = sum([portions[i] for i in candidates]), rest
        for i in candidates:
            more = min(most - given[i], max(1, remaining * portions[i] // pool), rest)
            given[i] = given[i] + more
            rest = rest - more
    return np.array(given)


def normal_values(own_key, dims, scale, most, cuts=(), kind=jnp.bfloat16):
    values = scale * jax.random.normal(own_key, dims, jnp.float32)
    if cuts:
        values = values * block_scale(own_key, dims, cuts, -0.22, 0.18)
    return jnp.clip(values, -most, most).astype(kind)


def setup_inputs(seed: int = 0, part: int = 0) -> dict:
    key_of = jax.random.split(jax.random.key(seed), 5)
    part_keys = jax.random.split(jax.random.fold_in(key_of[4], part), 5)
    tokens = draw_tokens(jax.random.fold_in(jax.random.fold_in(key_of[4], part), 71), part)
    out_grads = draw_out_grads(jax.random.fold_in(jax.random.fold_in(key_of[4], part), 71), part)
    routing_keys = jax.random.split(jax.random.fold_in(part_keys[2], 1), TOKENS // TOK_DEV)
    routing_turns = jax.random.permutation(jax.random.fold_in(part_keys[2], 3), TOKENS // TOK_DEV)
    routing = jax.vmap(lambda own, number: assign_block(jax.random.fold_in(part_keys[2], 2), own, number, TOK_DEV, E, 1, CAP, 1))(routing_keys, routing_turns).reshape((TOKENS, 1))
    weights = normal_values(part_keys[3], (E, D, F), 1.0, 6.0, ((1, 16),))
    return {"tokens": tokens, "out_grads": out_grads, "routing": routing, "weights": weights}


EPSILON = 1e-6


def reference(tokens, out_grads, routing, weights):
    token_sq = jnp.square(tokens.astype(jnp.float32))
    grad_sq = jnp.square(out_grads.astype(jnp.float32))
    labels = routing[:, 0].astype(jnp.int32)
    ranking = jnp.argsort(labels, stable=True).astype(jnp.int32)
    member = (labels[:, None] == jnp.arange(E, dtype=jnp.int32)[None, :]).astype(jnp.int32)
    counts = jnp.sum(member, axis=0).astype(jnp.int32)
    starts = (jnp.cumsum(counts) - counts).astype(jnp.int32)
    slot_span = N_TOK * CAP
    padded_tok = jnp.concatenate([token_sq[ranking], jnp.zeros((slot_span, D), token_sq.dtype)], axis=0)
    padded_grad = jnp.concatenate([grad_sq[ranking], jnp.zeros((slot_span, F), grad_sq.dtype)], axis=0)
    slot_ids = jnp.arange(slot_span, dtype=jnp.int32)

    def per_expert(expert):
        offset = starts[expert].astype(jnp.int32)
        live_mask = (slot_ids < counts[expert]).astype(token_sq.dtype)
        left_rows = lax.dynamic_slice_in_dim(padded_tok, offset, slot_span, 0) * live_mask[:, None]
        right_rows = lax.dynamic_slice_in_dim(padded_grad, offset, slot_span, 0)
        return lax.dot_general(left_rows, right_rows, (((0,), (0,)), ((), ())), precision=lax.Precision.HIGHEST)

    fisher_raw = lax.map(per_expert, jnp.arange(E, dtype=jnp.int32))
    totals = jnp.sum(fisher_raw, axis=(1, 2))
    scaling = totals / (D * F) + EPSILON
    fisher = fisher_raw / scaling[:, None, None]
    weights_wide = weights.astype(jnp.float32)
    merged = (jnp.sum(fisher * weights_wide, axis=0) / (jnp.sum(fisher, axis=0) + EPSILON)).astype(jnp.bfloat16)
    return (fisher, merged)
```

```python
import functools

import jax
import jax.numpy as jnp
from jax import lax
from jax.experimental import pallas as pl
from jax.experimental.pallas import tpu as pltpu
from jax.sharding import PartitionSpec as P

D = 7168
F = 1024
CAP = 48
EPSILON = 1e-06
GROUP = 8
TILE = 256


def summary_kernel(experts, cap, tok_ref, grad_ref, route_ref, out_ref):
    rows, width = tok_ref.shape
    member = (route_ref[...] == lax.broadcasted_iota(jnp.int32, (rows, 128), 1)).astype(jnp.float32)
    row_at = lax.broadcasted_iota(jnp.int32, (rows, rows), 0)
    col_at = lax.broadcasted_iota(jnp.int32, (rows, rows), 1)
    earlier = (col_at < row_at).astype(jnp.bfloat16)
    rank = jnp.dot(earlier, member.astype(jnp.bfloat16), preferred_element_type=jnp.float32)
    rank = jnp.sum(member * rank, axis=1, keepdims=True)
    slot = route_ref[...].astype(jnp.float32) * cap + rank
    tok = jnp.zeros((rows, 128), jnp.float32)
    for start in range(0, width, 128):
        tok = tok + jnp.square(tok_ref[:, start : start + 128].astype(jnp.float32))
    grad = jnp.zeros((rows, 128), jnp.float32)
    for start in range(0, grad_ref.shape[1], 128):
        grad = grad + jnp.square(grad_ref[:, start : start + 128].astype(jnp.float32))
    mass = jnp.sum(tok, axis=1, keepdims=True) * jnp.sum(grad, axis=1, keepdims=True)
    out_ref[...] = jnp.zeros_like(out_ref)
    out_ref[0:1, :] = jnp.sum(jnp.where(row_at == col_at, slot, 0.0), axis=0, keepdims=True)
    out_ref[1:2, :] = jnp.sum(member * mass, axis=0, keepdims=True)


def left_kernel(experts, cap, cols_ref, slot_ref, hi_ref, lo_ref):
    group, depth, rows = cols_ref.shape
    span = group * cap
    columns = jnp.concatenate([cols_ref[b] for b in range(group)], axis=1)
    lane = lax.broadcasted_iota(jnp.int32, (rows, span), 1).astype(jnp.float32)
    for expert in range(experts):
        picks = []
        for b in range(group):
            at = slot_ref[0, :, b : b + 1] - float(expert * cap)
            at = jnp.where((at >= 0.0) & (at < float(cap)), at + float(b * cap), -1.0)
            picks.append((at == lane).astype(jnp.bfloat16))
        placed = jnp.dot(columns, jnp.concatenate(picks, axis=0), preferred_element_type=jnp.float32)
        square = placed * placed
        hi = square.astype(jnp.bfloat16)
        hi_ref[expert] = hi
        lo_ref[expert] = (square - hi.astype(jnp.float32)).astype(jnp.bfloat16)


def merge_kernel(
    experts, cap, rows, scale_ref, slot_ref, hi_ref, lo_ref, grad_ref, weight_ref,
    fisher_ref, merged_ref, pick, right_hi, right_lo,
):
    blocks = slot_ref.shape[0]
    span = experts * cap

    @pl.when(pl.program_id(0) == 0)
    def _():
        at = lax.broadcasted_iota(jnp.int32, (span, rows), 0).astype(jnp.float32)
        for b in range(blocks):
            pick[b] = (slot_ref[b : b + 1, :] == at).astype(jnp.bfloat16)

    for b in range(blocks):
        placed = jnp.dot(
            pick[b], grad_ref[b * rows : (b + 1) * rows, :], preferred_element_type=jnp.float32
        )
        square = placed * placed
        hi = square.astype(jnp.bfloat16)
        lo = (square - hi.astype(jnp.float32)).astype(jnp.bfloat16)
        for expert in range(experts):
            right_hi[expert, b * cap : (b + 1) * cap, :] = hi[expert * cap : (expert + 1) * cap, :]
            right_lo[expert, b * cap : (b + 1) * cap, :] = lo[expert * cap : (expert + 1) * cap, :]

    dot = functools.partial(jnp.dot, preferred_element_type=jnp.float32)
    top = None
    bottom = None
    for expert in range(experts):
        raw = dot(hi_ref[expert], right_hi[expert])
        raw = raw + dot(hi_ref[expert], right_lo[expert])
        raw = raw + dot(lo_ref[expert], right_hi[expert])
        fisher = raw * scale_ref[expert]
        fisher_ref[expert] = fisher
        part = fisher * weight_ref[expert].astype(jnp.float32)
        top = part if top is None else top + part
        bottom = fisher if bottom is None else bottom + fisher
    merged_ref[...] = (top / (bottom + EPSILON)).astype(jnp.bfloat16)


def local(parts, tokens, out_grads, routing, weights):
    rows, width = tokens.shape
    experts, depth, hidden = weights.shape
    cap = min(rows, CAP)
    span = parts * cap
    gathered = lax.all_gather(out_grads, "tok", axis=0, tiled=True)
    turned = tokens.T.reshape(parts, depth, rows)
    columns = lax.all_to_all(turned, "tok", split_axis=0, concat_axis=0, tiled=True)

    summary = pl.pallas_call(
        functools.partial(summary_kernel, experts, cap),
        out_shape=jax.ShapeDtypeStruct((8, 128), jnp.float32),
        name="summary",
    )(tokens, out_grads, routing)
    summaries = lax.all_gather(summary[:2], "tok", axis=0)
    slots = summaries[:, 0, :]
    totals = jnp.sum(summaries[:, 1, :experts], axis=0)
    scale = 1.0 / (totals / (width * hidden) + EPSILON)

    groups = parts // GROUP
    left_hi, left_lo = pl.pallas_call(
        functools.partial(left_kernel, experts, cap),
        grid=(groups,),
        in_specs=[
            pl.BlockSpec((GROUP, depth, rows), lambda g: (g, 0, 0)),
            pl.BlockSpec((1, rows, GROUP), lambda g: (g, 0, 0)),
        ],
        out_specs=[pl.BlockSpec((experts, depth, GROUP * cap), lambda g: (0, 0, g))] * 2,
        out_shape=[jax.ShapeDtypeStruct((experts, depth, span), jnp.bfloat16)] * 2,
        compiler_params=pltpu.CompilerParams(vmem_limit_bytes=48 * 2**20),
        name="left",
    )(columns, jnp.swapaxes(slots.reshape(groups, GROUP, rows), 1, 2))

    whole = lambda *shape: pl.BlockSpec(shape, lambda f: (0,) * len(shape))
    fisher, merged = pl.pallas_call(
        functools.partial(merge_kernel, experts, cap, rows),
        grid=(hidden // TILE,),
        in_specs=[
            pl.BlockSpec(memory_space=pltpu.SMEM),
            whole(parts, rows),
            whole(experts, depth, span),
            whole(experts, depth, span),
            pl.BlockSpec((parts * rows, TILE), lambda f: (0, f)),
            pl.BlockSpec((experts, depth, TILE), lambda f: (0, 0, f)),
        ],
        out_specs=[
            pl.BlockSpec((experts, depth, TILE), lambda f: (0, 0, f)),
            pl.BlockSpec((depth, TILE), lambda f: (0, f)),
        ],
        out_shape=[
            jax.ShapeDtypeStruct((experts, depth, hidden), jnp.float32),
            jax.ShapeDtypeStruct((depth, hidden), jnp.bfloat16),
        ],
        scratch_shapes=[
            pltpu.VMEM((parts, experts * cap, rows), jnp.bfloat16),
            pltpu.VMEM((experts, span, TILE), jnp.bfloat16),
            pltpu.VMEM((experts, span, TILE), jnp.bfloat16),
        ],
        compiler_params=pltpu.CompilerParams(vmem_limit_bytes=48 * 2**20),
        name="merge",
    )(scale, slots, left_hi, left_lo, gathered, weights)
    return (fisher, merged)


def solution(mesh):
    in_specs = (
        P(("layer", "tok"), None),
        P(("layer", "tok"), None),
        P(("layer", "tok"), None),
        P("layer", "tok", None),
    )
    out_specs = (P("layer", "tok", None), P(("layer", "tok"), None))
    body = functools.partial(local, mesh.shape["tok"])
    return jax.shard_map(body, mesh=mesh, in_specs=in_specs, out_specs=out_specs, check_vma=False)
```

```python
import functools

import jax
import jax.numpy as jnp
from jax import lax
from jax.experimental import pallas as pl
from jax.experimental.pallas import tpu as pltpu
from jax.sharding import PartitionSpec as P

D = 7168
F = 1024
CAP = 48
EPSILON = 1e-06
TILE = 256


def parcel_kernel(experts, cap, tok_ref, grad_ref, route_ref, out_ref):
    rows, width = tok_ref.shape
    hidden = grad_ref.shape[1]
    expert_at = lax.broadcasted_iota(jnp.int32, (8, rows), 0)
    member = (route_ref[...] == expert_at).astype(jnp.float32)
    row_at = lax.broadcasted_iota(jnp.int32, (rows, rows), 0)
    col_at = lax.broadcasted_iota(jnp.int32, (rows, rows), 1)
    earlier = (row_at < col_at).astype(jnp.bfloat16)
    rank = jnp.dot(member.astype(jnp.bfloat16), earlier, preferred_element_type=jnp.float32)
    base = (expert_at * cap).astype(jnp.float32)
    slot = jnp.sum(member * (rank + base), axis=0, keepdims=True)
    tok = jnp.zeros((rows, 128), jnp.float32)
    for start in range(0, width, 128):
        tok = tok + jnp.square(tok_ref[:, start : start + 128].astype(jnp.float32))
    grad = jnp.zeros((rows, 128), jnp.float32)
    for start in range(0, hidden, 128):
        grad = grad + jnp.square(grad_ref[:, start : start + 128].astype(jnp.float32))
    mass = jnp.sum(tok, axis=1, keepdims=True) * jnp.sum(grad, axis=1, keepdims=True)
    mass = jnp.sum(jnp.where(row_at == col_at, mass, 0.0), axis=0, keepdims=True)
    total = jnp.sum(member * mass, axis=1, keepdims=True)
    high = total.astype(jnp.bfloat16).astype(jnp.float32)
    middle = (total - high).astype(jnp.bfloat16).astype(jnp.float32)
    lane = lax.broadcasted_iota(jnp.int32, (8, 128), 1)
    terms = jnp.where(lane == 0, high, jnp.where(lane == 1, middle, total - high - middle))
    note = jnp.concatenate([jnp.broadcast_to(slot, (8, rows)), terms], axis=0)
    out_ref[:rows, :] = grad_ref[...]
    out_ref[rows:, :] = jnp.zeros((16, hidden), jnp.bfloat16)
    out_ref[rows:, :128] = note.astype(jnp.bfloat16)


def split(value):
    square = value * value
    hi = square.astype(jnp.bfloat16)
    return hi, (square - hi.astype(jnp.float32)).astype(jnp.bfloat16)


def merge_kernel(
    experts, cap, order, me_ref, scale_ref, slot_ref, cols_any, weight_ref, *refs
):
    fisher_ref, merged_ref, left_hi, left_lo, right_hi, right_lo, pick, cols_ref, sem = refs[-9:]
    blocks = [ref.at[i] for ref in refs[:-9] for i in range(ref.shape[0])]
    parts, depth, rows = cols_ref.shape
    span = parts * cap

    @pl.when(pl.program_id(0) == 0)
    def _():
        me = me_ref[0]
        copy = pltpu.make_async_copy(cols_any, cols_ref, sem)
        copy.start()
        at = lax.broadcasted_iota(jnp.int32, (experts * cap, rows), 0).astype(jnp.float32)
        for place, block in enumerate(blocks):
            slot = block[rows : rows + 16, :rows].astype(jnp.float32)[0:1]
            pick[place] = (slot == at).astype(jnp.bfloat16)
        copy.wait()
        for start in range(0, span, TILE):
            first = start // cap
            last = -(-(start + TILE) // cap)
            columns = jnp.concatenate(
                [cols_ref[jnp.bitwise_xor(order[p], me)] for p in range(first, last)], axis=1
            )
            lane = lax.broadcasted_iota(jnp.int32, (rows, TILE), 1).astype(jnp.float32)
            for expert in range(experts):
                picks = []
                for p in range(first, last):
                    at = slot_ref[:, p : p + 1] - float(expert * cap)
                    real = (at >= 0.0) & (at < float(cap))
                    at = jnp.where(real, at + float(p * cap - start), -1.0)
                    picks.append((at == lane).astype(jnp.bfloat16))
                moved = jnp.dot(
                    columns, jnp.concatenate(picks, axis=0), preferred_element_type=jnp.float32
                )
                hi, lo = split(moved)
                left_hi[expert, :, start : start + TILE] = hi
                left_lo[expert, :, start : start + TILE] = lo

    for place, block in enumerate(blocks):
        moved = jnp.dot(pick[place], block[:rows, :], preferred_element_type=jnp.float32)
        hi, lo = split(moved)
        for expert in range(experts):
            own = slice(expert * cap, (expert + 1) * cap)
            at = slice(place * cap, (place + 1) * cap)
            right_hi[expert, at, :] = hi[own, :]
            right_lo[expert, at, :] = lo[own, :]

    dot = functools.partial(jnp.dot, preferred_element_type=jnp.float32)
    top = None
    bottom = None
    for expert in range(experts):
        raw = dot(left_hi[expert], right_hi[expert])
        raw = raw + dot(left_hi[expert], right_lo[expert])
        raw = raw + dot(left_lo[expert], right_hi[expert])
        fisher = raw * scale_ref[expert]
        fisher_ref[expert] = fisher
        part = fisher * weight_ref[expert].astype(jnp.float32)
        top = part if top is None else top + part
        bottom = fisher if bottom is None else bottom + fisher
    merged_ref[...] = (top / (bottom + EPSILON)).astype(jnp.bfloat16)


def local(parts, tokens, out_grads, routing, weights):
    rows, width = tokens.shape
    experts, depth, hidden = weights.shape
    cap = min(rows, CAP)
    span = parts * cap
    me = lax.axis_index("tok")

    def swap(value, flip):
        return lax.ppermute(value, "tok", [(s, s ^ flip) for s in range(parts)])

    turned = tokens.T.reshape(parts, depth, rows)
    parcel = pl.pallas_call(
        functools.partial(parcel_kernel, experts, cap),
        out_shape=jax.ShapeDtypeStruct((rows + 16, hidden), jnp.bfloat16),
        name="parcel",
    )(tokens, out_grads, routing.reshape(1, rows))

    if parts == 16:
        inward = [(s, s + 4) for s in range(4, 8)] + [(s, s - 4) for s in range(8, 12)]
        outward = [(s, s - 4) for s in range(4, 8)] + [(s, s + 4) for s in range(8, 12)]
        inner = (me // 4 == 1) | (me // 4 == 2)
        far = lax.ppermute(parcel, "tok", inward)
        near = swap(parcel, 4)
        far2 = lax.ppermute(near, "tok", inward)
        out = lax.ppermute(far, "tok", outward)
        out2 = lax.ppermute(far2, "tok", outward)
        pair = jnp.stack([parcel, near])
        across = swap(pair, 2)
        turned, pair, across, far, far2, out, out2 = lax.optimization_barrier(
            (turned, pair, across, far, far2, out, out2)
        )
        other = jnp.stack([jnp.where(inner, far, out2), jnp.where(inner, far2, out)])
        halves = [(pair, across, (0, 4)), (other, swap(other, 2), (12, 8))]
    else:
        near = swap(parcel, 4)
        pairs = [(jnp.stack([parcel, near]), (0, 4))]
        flip = 8
        while flip < parts:
            pairs = pairs + [(swap(b, flip), tuple(k ^ flip for k in ks)) for b, ks in pairs]
            flip *= 2
        halves = [(b, swap(b, 2), ks) for b, ks in pairs]
    columns = lax.all_to_all(turned, "tok", split_axis=0, concat_axis=0, tiled=True)

    order = []
    notes = []
    blocks = []
    for block, across, ks in halves:
        for b, flip in ((block, 0), (across, 2), (swap(block, 1), 1), (swap(across, 1), 3)):
            blocks.append(b)
            notes.append(b[:, rows:, :128].astype(jnp.float32))
            order += [k ^ flip for k in ks]

    notes = jnp.concatenate(notes)
    totals = jnp.sum(notes[:, 8 : 8 + experts, :3], axis=(0, 2))
    scale = 1.0 / (totals / (width * hidden) + EPSILON)
    slot_columns = notes[:, 0, :].T

    whole = lambda *shape: pl.BlockSpec(shape, lambda f: (0,) * len(shape))
    fisher, merged = pl.pallas_call(
        functools.partial(merge_kernel, experts, cap, tuple(order)),
        grid=(hidden // TILE,),
        in_specs=[
            pl.BlockSpec(memory_space=pltpu.SMEM),
            pl.BlockSpec(memory_space=pltpu.SMEM),
            whole(rows, parts),
            pl.BlockSpec(memory_space=pl.ANY),
            pl.BlockSpec((experts, depth, TILE), lambda f: (0, 0, f)),
        ]
        + [pl.BlockSpec((2, rows + 16, TILE), lambda f: (0, 0, f))] * len(blocks),
        out_specs=[
            pl.BlockSpec((experts, depth, TILE), lambda f: (0, 0, f)),
            pl.BlockSpec((depth, TILE), lambda f: (0, f)),
        ],
        out_shape=[
            jax.ShapeDtypeStruct((experts, depth, hidden), jnp.float32),
            jax.ShapeDtypeStruct((depth, hidden), jnp.bfloat16),
        ],
        scratch_shapes=[
            pltpu.VMEM((experts, depth, span), jnp.bfloat16),
            pltpu.VMEM((experts, depth, span), jnp.bfloat16),
            pltpu.VMEM((experts, span, TILE), jnp.bfloat16),
            pltpu.VMEM((experts, span, TILE), jnp.bfloat16),
            pltpu.VMEM((parts, experts * cap, rows), jnp.bfloat16),
            pltpu.VMEM((parts, depth, rows), jnp.bfloat16),
            pltpu.SemaphoreType.DMA,
        ],
        compiler_params=pltpu.CompilerParams(vmem_limit_bytes=60 * 2**20),
        name="merge",
    )(me.astype(jnp.int32)[None], scale, slot_columns, columns, weights, *blocks)
    return (fisher, merged)


def solution(mesh):
    in_specs = (
        P(("layer", "tok"), None),
        P(("layer", "tok"), None),
        P(("layer", "tok"), None),
        P("layer", "tok", None),
    )
    out_specs = (P("layer", "tok", None), P(("layer", "tok"), None))
    body = functools.partial(local, mesh.shape["tok"])
    return jax.shard_map(body, mesh=mesh, in_specs=in_specs, out_specs=out_specs, check_vma=False)
```

```python
import functools

import jax
import jax.numpy as jnp
from jax import lax
from jax.experimental import pallas as pl
from jax.experimental.pallas import tpu as pltpu
from jax.sharding import PartitionSpec as P

D = 7168
F = 1024
CAP = 48
EPSILON = 1e-06
TILE = 256


def turn_kernel(experts, cap, tok_ref, grad_ref, route_ref, turned_ref):
    rows, width = tok_ref.shape
    depth = width // turned_ref.shape[0]
    expert_at = lax.broadcasted_iota(jnp.int32, (8, rows), 0)
    member = (route_ref[...] == expert_at).astype(jnp.float32)
    row_at = lax.broadcasted_iota(jnp.int32, (rows, rows), 0)
    col_at = lax.broadcasted_iota(jnp.int32, (rows, rows), 1)
    earlier = (row_at < col_at).astype(jnp.bfloat16)
    rank = jnp.dot(member.astype(jnp.bfloat16), earlier, preferred_element_type=jnp.float32)
    base = (expert_at * cap).astype(jnp.float32)
    slot = jnp.sum(member * (rank + base), axis=0, keepdims=True)
    tok = jnp.zeros((rows, 128), jnp.float32)
    for start in range(0, width, 128):
        piece = tok_ref[:, start : start + 128]
        tok = tok + jnp.square(piece.astype(jnp.float32))
        down = piece.T
        at = start
        while at < start + 128:
            end = min(start + 128, (at // depth + 1) * depth)
            turned_ref[at // depth, at % depth : at % depth + end - at, :] = down[at - start : end - start]
            at = end
    grad = jnp.zeros((rows, 128), jnp.float32)
    for start in range(0, grad_ref.shape[1], 128):
        grad = grad + jnp.square(grad_ref[:, start : start + 128].astype(jnp.float32))
    mass = jnp.sum(tok, axis=1, keepdims=True) * jnp.sum(grad, axis=1, keepdims=True)
    mass = jnp.sum(jnp.where(row_at == col_at, mass, 0.0), axis=0, keepdims=True)
    total = jnp.sum(member * mass, axis=1, keepdims=True)
    high = total.astype(jnp.bfloat16).astype(jnp.float32)
    middle = (total - high).astype(jnp.bfloat16).astype(jnp.float32)
    lane = lax.broadcasted_iota(jnp.int32, (8, 128), 1)
    terms = jnp.where(lane == 1, middle, jnp.where(lane == 2, total - high - middle, 0.0))
    terms = jnp.where(lane == 0, high, terms)
    note = jnp.concatenate([jnp.broadcast_to(slot, (8, rows)), terms], axis=0)
    for part in range(turned_ref.shape[0]):
        turned_ref[part, depth:, :] = note.astype(jnp.bfloat16)


def split(value):
    square = value * value
    hi = square.astype(jnp.bfloat16)
    return hi, (square - hi.astype(jnp.float32)).astype(jnp.bfloat16)


def merge_kernel(experts, cap, order, count, me_ref, cols_any, weight_ref, *refs):
    fisher_ref, merged_ref, left_hi, left_lo, right_hi, right_lo = refs[-11:-5]
    pick, left_pick, scale_ref, cols_ref, sem = refs[-5:]
    blocks = [ref.at[i] for ref in refs[:-11] for i in range(ref.shape[0])]
    parts, tall, rows = cols_ref.shape
    depth = tall - 16
    span = parts * cap

    @pl.when(pl.program_id(0) == 0)
    def _():
        me = me_ref[0]
        copy = pltpu.make_async_copy(cols_any, cols_ref, sem)
        copy.start()
        copy.wait()
        at = lax.broadcasted_iota(jnp.int32, (experts * cap, rows), 0).astype(jnp.float32)
        total = jnp.zeros((8, rows), jnp.float32)
        for place in range(parts):
            note = cols_ref[jnp.bitwise_xor(order[place], me), depth:, :].astype(jnp.float32)
            pick[place] = (note[0:1] == at).astype(jnp.bfloat16)
            total = total + note[8:]
        total = jnp.sum(total, axis=1, keepdims=True)
        scale_ref[...] = jnp.broadcast_to(1.0 / (total / count + EPSILON), (8, 128))
        for start in range(0, span, TILE):
            left_pick[...] = jnp.zeros_like(left_pick)
            first = start // cap
            last = -(-(start + TILE) // cap)
            for p in range(first, last):
                low = max(p * cap, start)
                high = min((p + 1) * cap, start + TILE)
                for expert in range(experts):
                    slots = slice(low - p * cap + expert * cap, high - p * cap + expert * cap)
                    lanes = slice((p - first) * rows, (p - first + 1) * rows)
                    left_pick[expert, low - start : high - start, lanes] = pick[p, slots, :]
            columns = jnp.concatenate(
                [cols_ref[jnp.bitwise_xor(order[p], me), :depth, :] for p in range(first, last)], axis=1
            )
            for expert in range(experts):
                moved = lax.dot_general(
                    columns,
                    left_pick[expert, :, : (last - first) * rows],
                    (((1,), (1,)), ((), ())),
                    preferred_element_type=jnp.float32,
                )
                hi, lo = split(moved)
                left_hi[expert, :, start : start + TILE] = hi
                left_lo[expert, :, start : start + TILE] = lo

    for place, block in enumerate(blocks):
        moved = jnp.dot(pick[place], block[...], preferred_element_type=jnp.float32)
        hi, lo = split(moved)
        for expert in range(experts):
            own = slice(expert * cap, (expert + 1) * cap)
            at = slice(place * cap, (place + 1) * cap)
            right_hi[expert, at, :] = hi[own, :]
            right_lo[expert, at, :] = lo[own, :]

    dot = functools.partial(jnp.dot, preferred_element_type=jnp.float32)
    top = None
    bottom = None
    for expert in range(experts):
        raw = dot(left_hi[expert], right_hi[expert])
        raw = raw + dot(left_hi[expert], right_lo[expert])
        raw = raw + dot(left_lo[expert], right_hi[expert])
        fisher = raw * scale_ref[expert : expert + 1, 0:1]
        fisher_ref[expert] = fisher
        part = fisher * weight_ref[expert].astype(jnp.float32)
        top = part if top is None else top + part
        bottom = fisher if bottom is None else bottom + fisher
    merged_ref[...] = (top / (bottom + EPSILON)).astype(jnp.bfloat16)


def local(parts, tokens, out_grads, routing, weights):
    rows, width = tokens.shape
    experts, depth, hidden = weights.shape
    cap = min(rows, CAP)
    span = parts * cap
    me = lax.axis_index("tok")

    def swap(value, flip):
        return lax.ppermute(value, "tok", [(s, s ^ flip) for s in range(parts)])

    turned = pl.pallas_call(
        functools.partial(turn_kernel, experts, cap),
        out_shape=pltpu.HBM((parts, depth + 16, rows), jnp.bfloat16),
        compiler_params=pltpu.CompilerParams(vmem_limit_bytes=16 * 2**20),
        name="turn",
    )(tokens, out_grads, routing.reshape(1, rows))

    if parts == 16:
        inward = [(s, s + 4) for s in range(4, 8)] + [(s, s - 4) for s in range(8, 12)]
        outward = [(s, s - 4) for s in range(4, 8)] + [(s, s + 4) for s in range(8, 12)]
        inner = (me // 4 == 1) | (me // 4 == 2)
        far = lax.ppermute(out_grads, "tok", inward)
        near = swap(out_grads, 4)
        far2 = lax.ppermute(near, "tok", inward)
        out = lax.ppermute(far, "tok", outward)
        pair = jnp.stack([out_grads, near])
        across = swap(pair, 2)
        out2 = lax.ppermute(far2, "tok", outward)
        turned, pair, across, far, far2, out, out2 = lax.optimization_barrier(
            (turned, pair, across, far, far2, out, out2)
        )
        other = jnp.stack([jnp.where(inner, far, out2), jnp.where(inner, far2, out)])
        halves = [(pair, across, (0, 4)), (other, swap(other, 2), (12, 8))]
    else:
        near = swap(out_grads, 4)
        pairs = [(jnp.stack([out_grads, near]), (0, 4))]
        flip = 8
        while flip < parts:
            pairs = pairs + [(swap(b, flip), tuple(k ^ flip for k in ks)) for b, ks in pairs]
            flip *= 2
        halves = [(b, swap(b, 2), ks) for b, ks in pairs]
    columns = lax.all_to_all(turned, "tok", split_axis=0, concat_axis=0, tiled=True)

    order = []
    blocks = []
    for block, across, ks in halves:
        for b, flip in ((block, 0), (across, 2), (swap(block, 1), 1), (swap(across, 1), 3)):
            blocks.append(b)
            order += [k ^ flip for k in ks]

    fisher, merged = pl.pallas_call(
        functools.partial(merge_kernel, experts, cap, tuple(order), width * hidden),
        grid=(hidden // TILE,),
        in_specs=[
            pl.BlockSpec(memory_space=pltpu.SMEM),
            pl.BlockSpec(memory_space=pl.ANY),
            pl.BlockSpec((experts, depth, TILE), lambda f: (0, 0, f)),
        ]
        + [pl.BlockSpec((2, rows, TILE), lambda f: (0, 0, f))] * len(blocks),
        out_specs=[
            pl.BlockSpec((experts, depth, TILE), lambda f: (0, 0, f)),
            pl.BlockSpec((depth, TILE), lambda f: (0, f)),
        ],
        out_shape=[
            jax.ShapeDtypeStruct((experts, depth, hidden), jnp.float32),
            jax.ShapeDtypeStruct((depth, hidden), jnp.bfloat16),
        ],
        scratch_shapes=[
            pltpu.VMEM((experts, depth, span), jnp.bfloat16),
            pltpu.VMEM((experts, depth, span), jnp.bfloat16),
            pltpu.VMEM((experts, span, TILE), jnp.bfloat16),
            pltpu.VMEM((experts, span, TILE), jnp.bfloat16),
            pltpu.VMEM((parts, experts * cap, rows), jnp.bfloat16),
            pltpu.VMEM((experts, TILE, (-(-TILE // cap) + 1) * rows), jnp.bfloat16),
            pltpu.VMEM((8, 128), jnp.float32),
            pltpu.VMEM((parts, depth + 16, rows), jnp.bfloat16),
            pltpu.SemaphoreType.DMA,
        ],
        compiler_params=pltpu.CompilerParams(vmem_limit_bytes=60 * 2**20),
        name="merge",
    )(me.astype(jnp.int32)[None], columns, weights, *blocks)
    return (fisher, merged)


def solution(mesh):
    in_specs = (
        P(("layer", "tok"), None),
        P(("layer", "tok"), None),
        P(("layer", "tok"), None),
        P("layer", "tok", None),
    )
    out_specs = (P("layer", "tok", None), P(("layer", "tok"), None))
    body = functools.partial(local, mesh.shape["tok"])
    return jax.shard_map(body, mesh=mesh, in_specs=in_specs, out_specs=out_specs, check_vma=False)
```

```python
import functools

import jax
import jax.numpy as jnp
from jax import lax
from jax.experimental import pallas as pl
from jax.experimental.pallas import tpu as pltpu
from jax.sharding import PartitionSpec as P

D = 7168
F = 1024
CAP = 48
EPSILON = 1e-06
TILE = 256


def turn_kernel(experts, cap, tok_ref, grad_ref, route_ref, turned_ref):
    rows, width = tok_ref.shape
    depth = width // turned_ref.shape[0]
    expert_at = lax.broadcasted_iota(jnp.int32, (8, rows), 0)
    member = (route_ref[...] == expert_at).astype(jnp.float32)
    row_at = lax.broadcasted_iota(jnp.int32, (rows, rows), 0)
    col_at = lax.broadcasted_iota(jnp.int32, (rows, rows), 1)
    earlier = (row_at < col_at).astype(jnp.bfloat16)
    rank = jnp.dot(member.astype(jnp.bfloat16), earlier, preferred_element_type=jnp.float32)
    base = (expert_at * cap).astype(jnp.float32)
    slot = jnp.sum(member * (rank + base), axis=0, keepdims=True)
    tok = jnp.zeros((rows, 128), jnp.float32)
    for start in range(0, width, 128):
        piece = tok_ref[:, start : start + 128]
        tok = tok + jnp.square(piece.astype(jnp.float32))
        down = piece.T
        at = start
        while at < start + 128:
            end = min(start + 128, (at // depth + 1) * depth)
            turned_ref[at // depth, at % depth : at % depth + end - at, :] = down[at - start : end - start]
            at = end
    grad = jnp.zeros((rows, 128), jnp.float32)
    for start in range(0, grad_ref.shape[1], 128):
        grad = grad + jnp.square(grad_ref[:, start : start + 128].astype(jnp.float32))
    mass = jnp.sum(tok, axis=1, keepdims=True) * jnp.sum(grad, axis=1, keepdims=True)
    mass = jnp.sum(jnp.where(row_at == col_at, mass, 0.0), axis=0, keepdims=True)
    total = jnp.sum(member * mass, axis=1, keepdims=True)
    high = total.astype(jnp.bfloat16).astype(jnp.float32)
    middle = (total - high).astype(jnp.bfloat16).astype(jnp.float32)
    lane = lax.broadcasted_iota(jnp.int32, (8, 128), 1)
    terms = jnp.where(lane == 1, middle, jnp.where(lane == 2, total - high - middle, 0.0))
    terms = jnp.where(lane == 0, high, terms)
    note = jnp.concatenate([jnp.broadcast_to(slot, (8, rows)), terms], axis=0)
    for part in range(turned_ref.shape[0]):
        turned_ref[part, depth:, :] = note.astype(jnp.bfloat16)


def split(value):
    square = value * value
    hi = square.astype(jnp.bfloat16)
    return hi, (square - hi.astype(jnp.float32)).astype(jnp.bfloat16)


def merge_kernel(experts, cap, order, count, me_ref, cols_any, weight_ref, *refs):
    fisher_ref, merged_ref, left_hi, left_lo, right_hi, right_lo = refs[-11:-5]
    pick, left_pick, scale_ref, cols_ref, sem = refs[-5:]
    blocks = refs[:-11]
    parts, tall, rows = cols_ref.shape
    depth = tall - 16
    span = parts * cap

    @pl.when(pl.program_id(0) == 0)
    def _():
        me = me_ref[0]
        copy = pltpu.make_async_copy(cols_any, cols_ref, sem)
        copy.start()
        copy.wait()
        at = lax.broadcasted_iota(jnp.int32, (experts * cap, rows), 0).astype(jnp.float32)
        total = jnp.zeros((8, rows), jnp.float32)
        for place in range(parts):
            note = cols_ref[jnp.bitwise_xor(order[place], me), depth:, :].astype(jnp.float32)
            pick[place] = (note[0:1] == at).astype(jnp.bfloat16)
            total = total + note[8:]
        total = jnp.sum(total, axis=1, keepdims=True)
        scale_ref[...] = jnp.broadcast_to(1.0 / (total / count + EPSILON), (8, 128))
        for start in range(0, span, TILE):
            left_pick[...] = jnp.zeros_like(left_pick)
            first = start // cap
            last = -(-(start + TILE) // cap)
            for p in range(first, last):
                low = max(p * cap, start)
                high = min((p + 1) * cap, start + TILE)
                for expert in range(experts):
                    slots = slice(low - p * cap + expert * cap, high - p * cap + expert * cap)
                    lanes = slice((p - first) * rows, (p - first + 1) * rows)
                    left_pick[expert, low - start : high - start, lanes] = pick[p, slots, :]
            columns = jnp.concatenate(
                [cols_ref[jnp.bitwise_xor(order[p], me), :depth, :] for p in range(first, last)], axis=1
            )
            for expert in range(experts):
                moved = lax.dot_general(
                    columns,
                    left_pick[expert, :, : (last - first) * rows],
                    (((1,), (1,)), ((), ())),
                    preferred_element_type=jnp.float32,
                )
                hi, lo = split(moved)
                left_hi[expert, :, start : start + TILE] = hi
                left_lo[expert, :, start : start + TILE] = lo

    for place, block in enumerate(blocks):
        moved = jnp.dot(pick[place], block[...], preferred_element_type=jnp.float32)
        hi, lo = split(moved)
        for expert in range(experts):
            own = slice(expert * cap, (expert + 1) * cap)
            at = slice(place * cap, (place + 1) * cap)
            right_hi[expert, at, :] = hi[own, :]
            right_lo[expert, at, :] = lo[own, :]

    dot = functools.partial(jnp.dot, preferred_element_type=jnp.float32)
    top = None
    bottom = None
    for expert in range(experts):
        raw = dot(left_hi[expert], right_hi[expert])
        raw = raw + dot(left_hi[expert], right_lo[expert])
        raw = raw + dot(left_lo[expert], right_hi[expert])
        fisher = raw * scale_ref[expert : expert + 1, 0:1]
        fisher_ref[expert] = fisher
        part = fisher * weight_ref[expert].astype(jnp.float32)
        top = part if top is None else top + part
        bottom = fisher if bottom is None else bottom + fisher
    merged_ref[...] = (top / (bottom + EPSILON)).astype(jnp.bfloat16)


def local(parts, tokens, out_grads, routing, weights):
    rows, width = tokens.shape
    experts, depth, hidden = weights.shape
    cap = min(rows, CAP)
    span = parts * cap
    me = lax.axis_index("tok")

    def swap(value, flip):
        return lax.ppermute(value, "tok", [(s, s ^ flip) for s in range(parts)])

    turned = pl.pallas_call(
        functools.partial(turn_kernel, experts, cap),
        out_shape=pltpu.HBM((parts, depth + 16, rows), jnp.bfloat16),
        compiler_params=pltpu.CompilerParams(vmem_limit_bytes=16 * 2**20),
        name="turn",
    )(tokens, out_grads, routing.reshape(1, rows))

    held = {0: out_grads}
    if parts == 16:
        inward = [(s, s + 4) for s in range(4, 8)] + [(s, s - 4) for s in range(8, 12)]
        outward = [(s, s - 4) for s in range(4, 8)] + [(s, s + 4) for s in range(8, 12)]
        inner = (me // 4 == 1) | (me // 4 == 2)
        y_own = swap(out_grads, 2)
        near = swap(out_grads, 4)
        second = swap(out_grads, 8)
        y_own, near, second = lax.optimization_barrier((y_own, near, second))
        far = lax.ppermute(out_grads, "tok", inward)
        out = lax.ppermute(second, "tok", outward)
        y_near = swap(near, 2)
        (turned, far, out) = lax.optimization_barrier(
            (turned, far, out)
        )
        third = jnp.where(inner, far, out)
        y_second = swap(second, 2)
        held.update({4: near, 8: second, 12: third})
        held.update({2: y_own, 6: y_near, 10: y_second, 14: swap(third, 2)})
    else:
        flip = parts // 2
        while flip > 1:
            held.update({k ^ flip: swap(b, flip) for k, b in held.items()})
            flip //= 2
    held.update({k ^ 1: swap(b, 1) for k, b in held.items()})
    order = sorted(held)
    blocks = [held[k] for k in order]

    columns = lax.all_to_all(turned, "tok", split_axis=0, concat_axis=0, tiled=True)

    fisher, merged = pl.pallas_call(
        functools.partial(merge_kernel, experts, cap, tuple(order), width * hidden),
        grid=(hidden // TILE,),
        in_specs=[
            pl.BlockSpec(memory_space=pltpu.SMEM),
            pl.BlockSpec(memory_space=pl.ANY),
            pl.BlockSpec((experts, depth, TILE), lambda f: (0, 0, f)),
        ]
        + [pl.BlockSpec((rows, TILE), lambda f: (0, f))] * len(blocks),
        out_specs=[
            pl.BlockSpec((experts, depth, TILE), lambda f: (0, 0, f)),
            pl.BlockSpec((depth, TILE), lambda f: (0, f)),
        ],
        out_shape=[
            jax.ShapeDtypeStruct((experts, depth, hidden), jnp.float32),
            jax.ShapeDtypeStruct((depth, hidden), jnp.bfloat16),
        ],
        scratch_shapes=[
            pltpu.VMEM((experts, depth, span), jnp.bfloat16),
            pltpu.VMEM((experts, depth, span), jnp.bfloat16),
            pltpu.VMEM((experts, span, TILE), jnp.bfloat16),
            pltpu.VMEM((experts, span, TILE), jnp.bfloat16),
            pltpu.VMEM((parts, experts * cap, rows), jnp.bfloat16),
            pltpu.VMEM((experts, TILE, (-(-TILE // cap) + 1) * rows), jnp.bfloat16),
            pltpu.VMEM((8, 128), jnp.float32),
            pltpu.VMEM((parts, depth + 16, rows), jnp.bfloat16),
            pltpu.SemaphoreType.DMA,
        ],
        compiler_params=pltpu.CompilerParams(vmem_limit_bytes=60 * 2**20),
        name="merge",
    )(me.astype(jnp.int32)[None], columns, weights, *blocks)
    return (fisher, merged)


def solution(mesh):
    in_specs = (
        P(("layer", "tok"), None),
        P(("layer", "tok"), None),
        P(("layer", "tok"), None),
        P("layer", "tok", None),
    )
    out_specs = (P("layer", "tok", None), P(("layer", "tok"), None))
    body = functools.partial(local, mesh.shape["tok"])
    return jax.shard_map(body, mesh=mesh, in_specs=in_specs, out_specs=out_specs, check_vma=False)
```

```python
import functools

import jax
import jax.numpy as jnp
from jax import lax
from jax.experimental import pallas as pl
from jax.experimental.pallas import tpu as pltpu
from jax.sharding import PartitionSpec as P

D = 7168
F = 1024
CAP = 48
EPSILON = 1e-06
TILE = 256


def turn_kernel(experts, cap, tok_ref, grad_ref, route_ref, turned_ref):
    rows, width = tok_ref.shape
    depth = width // turned_ref.shape[0]
    expert_at = lax.broadcasted_iota(jnp.int32, (8, rows), 0)
    member = (route_ref[...] == expert_at).astype(jnp.float32)
    row_at = lax.broadcasted_iota(jnp.int32, (rows, rows), 0)
    col_at = lax.broadcasted_iota(jnp.int32, (rows, rows), 1)
    earlier = (row_at < col_at).astype(jnp.bfloat16)
    rank = jnp.dot(member.astype(jnp.bfloat16), earlier, preferred_element_type=jnp.float32)
    base = (expert_at * cap).astype(jnp.float32)
    slot = jnp.sum(member * (rank + base), axis=0, keepdims=True)
    tok = jnp.zeros((rows, 128), jnp.float32)
    for start in range(0, width, 128):
        piece = tok_ref[:, start : start + 128]
        tok = tok + jnp.square(piece.astype(jnp.float32))
        down = piece.T
        at = start
        while at < start + 128:
            end = min(start + 128, (at // depth + 1) * depth)
            turned_ref[at // depth, at % depth : at % depth + end - at, :] = down[at - start : end - start]
            at = end
    grad = jnp.zeros((rows, 128), jnp.float32)
    for start in range(0, grad_ref.shape[1], 128):
        grad = grad + jnp.square(grad_ref[:, start : start + 128].astype(jnp.float32))
    mass = jnp.sum(tok, axis=1, keepdims=True) * jnp.sum(grad, axis=1, keepdims=True)
    mass = jnp.sum(jnp.where(row_at == col_at, mass, 0.0), axis=0, keepdims=True)
    total = jnp.sum(member * mass, axis=1, keepdims=True)
    high = total.astype(jnp.bfloat16).astype(jnp.float32)
    middle = (total - high).astype(jnp.bfloat16).astype(jnp.float32)
    lane = lax.broadcasted_iota(jnp.int32, (8, 128), 1)
    terms = jnp.where(lane == 1, middle, jnp.where(lane == 2, total - high - middle, 0.0))
    terms = jnp.where(lane == 0, high, terms)
    note = jnp.concatenate([jnp.broadcast_to(slot, (8, rows)), terms], axis=0)
    for part in range(turned_ref.shape[0]):
        turned_ref[part, depth:, :] = note.astype(jnp.bfloat16)


def split(value):
    square = value * value
    hi = square.astype(jnp.bfloat16)
    return hi, (square - hi.astype(jnp.float32)).astype(jnp.bfloat16)


def merge_kernel(experts, cap, order, count, me_ref, cols_ref, weight_ref, *refs):
    fisher_ref, merged_ref, left_hi, left_lo, right_hi, right_lo = refs[-9:-3]
    pick, left_pick, scale_ref = refs[-3:]
    blocks = refs[:-9]
    parts, tall, rows = cols_ref.shape
    depth = tall - 16
    span = parts * cap

    @pl.when(pl.program_id(0) == 0)
    def _():
        me = me_ref[0]
        at = lax.broadcasted_iota(jnp.int32, (experts * cap, rows), 0).astype(jnp.float32)
        total = jnp.zeros((8, rows), jnp.float32)
        for place in range(parts):
            note = cols_ref[jnp.bitwise_xor(order[place], me), depth:, :].astype(jnp.float32)
            pick[place] = (note[0:1] == at).astype(jnp.bfloat16)
            total = total + note[8:]
        total = jnp.sum(total, axis=1, keepdims=True)
        scale_ref[...] = jnp.broadcast_to(1.0 / (total / count + EPSILON), (8, 128))
        for start in range(0, span, TILE):
            left_pick[...] = jnp.zeros_like(left_pick)
            first = start // cap
            last = -(-(start + TILE) // cap)
            for p in range(first, last):
                low = max(p * cap, start)
                high = min((p + 1) * cap, start + TILE)
                for expert in range(experts):
                    slots = slice(low - p * cap + expert * cap, high - p * cap + expert * cap)
                    lanes = slice((p - first) * rows, (p - first + 1) * rows)
                    left_pick[expert, low - start : high - start, lanes] = pick[p, slots, :]
            columns = jnp.concatenate(
                [cols_ref[jnp.bitwise_xor(order[p], me), :depth, :] for p in range(first, last)], axis=1
            )
            for expert in range(experts):
                moved = lax.dot_general(
                    columns,
                    left_pick[expert, :, : (last - first) * rows],
                    (((1,), (1,)), ((), ())),
                    preferred_element_type=jnp.float32,
                )
                hi, lo = split(moved)
                left_hi[expert, :, start : start + TILE] = hi
                left_lo[expert, :, start : start + TILE] = lo

    for place, block in enumerate(blocks):
        moved = jnp.dot(pick[place], block[...], preferred_element_type=jnp.float32)
        hi, lo = split(moved)
        for expert in range(experts):
            own = slice(expert * cap, (expert + 1) * cap)
            at = slice(place * cap, (place + 1) * cap)
            right_hi[expert, at, :] = hi[own, :]
            right_lo[expert, at, :] = lo[own, :]

    dot = functools.partial(jnp.dot, preferred_element_type=jnp.float32)
    top = None
    bottom = None
    for expert in range(experts):
        raw = dot(left_hi[expert], right_hi[expert])
        raw = raw + dot(left_hi[expert], right_lo[expert])
        raw = raw + dot(left_lo[expert], right_hi[expert])
        fisher = raw * scale_ref[expert : expert + 1, 0:1]
        fisher_ref[expert] = fisher
        part = fisher * weight_ref[expert].astype(jnp.float32)
        top = part if top is None else top + part
        bottom = fisher if bottom is None else bottom + fisher
    merged_ref[...] = (top / (bottom + EPSILON)).astype(jnp.bfloat16)


def local(parts, tokens, out_grads, routing, weights):
    rows, width = tokens.shape
    experts, depth, hidden = weights.shape
    cap = min(rows, CAP)
    span = parts * cap
    me = lax.axis_index("tok")

    def swap(value, flip):
        return lax.ppermute(value, "tok", [(s, s ^ flip) for s in range(parts)])

    turned = pl.pallas_call(
        functools.partial(turn_kernel, experts, cap),
        out_shape=pltpu.HBM((parts, depth + 16, rows), jnp.bfloat16),
        compiler_params=pltpu.CompilerParams(vmem_limit_bytes=16 * 2**20),
        name="turn",
    )(tokens, out_grads, routing.reshape(1, rows))

    held = {0: out_grads}
    if parts == 16:
        inward = [(s, s + 4) for s in range(4, 8)] + [(s, s - 4) for s in range(8, 12)]
        outward = [(s, s - 4) for s in range(4, 8)] + [(s, s + 4) for s in range(8, 12)]
        inner = (me // 4 == 1) | (me // 4 == 2)
        y_own = swap(out_grads, 2)
        near = swap(out_grads, 4)
        second = swap(out_grads, 8)
        y_own, near, second = lax.optimization_barrier((y_own, near, second))
        far = lax.ppermute(out_grads, "tok", inward)
        out = lax.ppermute(second, "tok", outward)
        y_near = swap(near, 2)
        (turned, far, out) = lax.optimization_barrier(
            (turned, far, out)
        )
        third = jnp.where(inner, far, out)
        y_second = swap(second, 2)
        held.update({4: near, 8: second, 12: third})
        held.update({2: y_own, 6: y_near, 10: y_second, 14: swap(third, 2)})
    else:
        flip = parts // 2
        while flip > 1:
            held.update({k ^ flip: swap(b, flip) for k, b in held.items()})
            flip //= 2
    held.update({k ^ 1: swap(b, 1) for k, b in held.items()})
    order = sorted(held)
    blocks = [held[k] for k in order]

    columns = lax.all_to_all(turned, "tok", split_axis=0, concat_axis=0, tiled=True)

    fisher, merged = pl.pallas_call(
        functools.partial(merge_kernel, experts, cap, tuple(order), width * hidden),
        grid=(hidden // TILE,),
        in_specs=[
            pl.BlockSpec(memory_space=pltpu.SMEM),
            pl.BlockSpec((parts, depth + 16, rows), lambda f: (0, 0, 0), pipeline_mode=pl.Buffered(1)),
            pl.BlockSpec((experts, depth, TILE), lambda f: (0, 0, f)),
        ]
        + [pl.BlockSpec((rows, TILE), lambda f: (0, f))] * len(blocks),
        out_specs=[
            pl.BlockSpec((experts, depth, TILE), lambda f: (0, 0, f)),
            pl.BlockSpec((depth, TILE), lambda f: (0, f)),
        ],
        out_shape=[
            jax.ShapeDtypeStruct((experts, depth, hidden), jnp.float32),
            jax.ShapeDtypeStruct((depth, hidden), jnp.bfloat16),
        ],
        scratch_shapes=[
            pltpu.VMEM((experts, depth, span), jnp.bfloat16),
            pltpu.VMEM((experts, depth, span), jnp.bfloat16),
            pltpu.VMEM((experts, span, TILE), jnp.bfloat16),
            pltpu.VMEM((experts, span, TILE), jnp.bfloat16),
            pltpu.VMEM((parts, experts * cap, rows), jnp.bfloat16),
            pltpu.VMEM((experts, TILE, (-(-TILE // cap) + 1) * rows), jnp.bfloat16),
            pltpu.VMEM((8, 128), jnp.float32),
        ],
        compiler_params=pltpu.CompilerParams(vmem_limit_bytes=60 * 2**20),
        name="merge",
    )(me.astype(jnp.int32)[None], columns, weights, *blocks)
    return (fisher, merged)


def solution(mesh):
    in_specs = (
        P(("layer", "tok"), None),
        P(("layer", "tok"), None),
        P(("layer", "tok"), None),
        P("layer", "tok", None),
    )
    out_specs = (P("layer", "tok", None), P(("layer", "tok"), None))
    body = functools.partial(local, mesh.shape["tok"])
    return jax.shard_map(body, mesh=mesh, in_specs=in_specs, out_specs=out_specs, check_vma=False)
```

```python
import functools

import jax
import jax.numpy as jnp
from jax import lax
from jax.experimental import pallas as pl
from jax.experimental.pallas import tpu as pltpu
from jax.sharding import PartitionSpec as P

D = 7168
F = 1024
CAP = 48
EPSILON = 1e-06
TILE = 256


def turn_kernel(experts, cap, tok_ref, grad_ref, route_ref, turned_ref):
    rows, width = tok_ref.shape
    depth = width // turned_ref.shape[0]
    expert_at = lax.broadcasted_iota(jnp.int32, (8, rows), 0)
    member = (route_ref[...] == expert_at).astype(jnp.float32)
    row_at = lax.broadcasted_iota(jnp.int32, (rows, rows), 0)
    col_at = lax.broadcasted_iota(jnp.int32, (rows, rows), 1)
    earlier = (row_at < col_at).astype(jnp.bfloat16)
    rank = jnp.dot(member.astype(jnp.bfloat16), earlier, preferred_element_type=jnp.float32)
    base = (expert_at * cap).astype(jnp.float32)
    slot = jnp.sum(member * (rank + base), axis=0, keepdims=True)
    tok = jnp.zeros((rows, 128), jnp.float32)
    for start in range(0, width, 128):
        piece = tok_ref[:, start : start + 128]
        tok = tok + jnp.square(piece.astype(jnp.float32))
        down = piece.T
        at = start
        while at < start + 128:
            end = min(start + 128, (at // depth + 1) * depth)
            turned_ref[at // depth, at % depth : at % depth + end - at, :] = down[at - start : end - start]
            at = end
    grad = jnp.zeros((rows, 128), jnp.float32)
    for start in range(0, grad_ref.shape[1], 128):
        grad = grad + jnp.square(grad_ref[:, start : start + 128].astype(jnp.float32))
    mass = jnp.sum(tok, axis=1, keepdims=True) * jnp.sum(grad, axis=1, keepdims=True)
    mass = jnp.sum(jnp.where(row_at == col_at, mass, 0.0), axis=0, keepdims=True)
    total = jnp.sum(member * mass, axis=1, keepdims=True)
    high = total.astype(jnp.bfloat16).astype(jnp.float32)
    middle = (total - high).astype(jnp.bfloat16).astype(jnp.float32)
    lane = lax.broadcasted_iota(jnp.int32, (8, 128), 1)
    terms = jnp.where(lane == 1, middle, jnp.where(lane == 2, total - high - middle, 0.0))
    terms = jnp.where(lane == 0, high, terms)
    note = jnp.concatenate([jnp.broadcast_to(slot, (8, rows)), terms], axis=0)
    for part in range(turned_ref.shape[0]):
        turned_ref[part, depth:, :] = note.astype(jnp.bfloat16)


def split(value):
    square = value * value
    hi = square.astype(jnp.bfloat16)
    return hi, (square - hi.astype(jnp.float32)).astype(jnp.bfloat16)


def merge_kernel(experts, cap, order, count, me_ref, cols_ref, weight_ref, *refs):
    fisher_ref, merged_ref, left_hi, left_lo, right_hi, right_lo = refs[-9:-3]
    pick, left_pick, scale_ref = refs[-3:]
    blocks = refs[:-9]
    parts, tall, rows = cols_ref.shape
    depth = tall - 16
    span = parts * cap

    @pl.when(pl.program_id(0) == 0)
    def _():
        me = me_ref[0]
        at = lax.broadcasted_iota(jnp.int32, (experts * cap, rows), 0).astype(jnp.float32)
        total = jnp.zeros((8, rows), jnp.float32)
        for place in range(parts):
            note = cols_ref[jnp.bitwise_xor(order[place], me), depth:, :].astype(jnp.float32)
            pick[place] = (note[0:1] == at).astype(jnp.bfloat16)
            total = total + note[8:]
        total = jnp.sum(total, axis=1, keepdims=True)
        scale_ref[...] = jnp.broadcast_to(1.0 / (total / count + EPSILON), (8, 128))
        for start in range(0, span, TILE):
            left_pick[...] = jnp.zeros_like(left_pick)
            first = start // cap
            last = -(-(start + TILE) // cap)
            for p in range(first, last):
                low = max(p * cap, start)
                high = min((p + 1) * cap, start + TILE)
                for expert in range(experts):
                    slots = slice(low - p * cap + expert * cap, high - p * cap + expert * cap)
                    lanes = slice((p - first) * rows, (p - first + 1) * rows)
                    left_pick[expert, low - start : high - start, lanes] = pick[p, slots, :]
            columns = jnp.concatenate(
                [cols_ref[jnp.bitwise_xor(order[p], me), :depth, :] for p in range(first, last)], axis=1
            )
            for expert in range(experts):
                moved = lax.dot_general(
                    columns,
                    left_pick[expert, :, : (last - first) * rows],
                    (((1,), (1,)), ((), ())),
                    preferred_element_type=jnp.float32,
                )
                hi, lo = split(moved)
                left_hi[expert, :, start : start + TILE] = hi
                left_lo[expert, :, start : start + TILE] = lo

    for place, block in enumerate(blocks):
        moved = jnp.dot(pick[place], block[...], preferred_element_type=jnp.float32)
        hi, lo = split(moved)
        for expert in range(experts):
            own = slice(expert * cap, (expert + 1) * cap)
            at = slice(place * cap, (place + 1) * cap)
            right_hi[expert, at, :] = hi[own, :]
            right_lo[expert, at, :] = lo[own, :]

    dot = functools.partial(jnp.dot, preferred_element_type=jnp.float32)
    top = None
    bottom = None
    for expert in range(experts):
        raw = dot(left_hi[expert], right_hi[expert])
        raw = raw + dot(left_hi[expert], right_lo[expert])
        raw = raw + dot(left_lo[expert], right_hi[expert])
        fisher = raw * scale_ref[expert : expert + 1, 0:1]
        fisher_ref[expert] = fisher
        part = fisher * weight_ref[expert].astype(jnp.float32)
        top = part if top is None else top + part
        bottom = fisher if bottom is None else bottom + fisher
    merged_ref[...] = (top / (bottom + EPSILON)).astype(jnp.bfloat16)


def local(parts, tokens, out_grads, routing, weights):
    rows, width = tokens.shape
    experts, depth, hidden = weights.shape
    cap = min(rows, CAP)
    span = parts * cap
    me = lax.axis_index("tok")

    def swap(value, flip):
        return lax.ppermute(value, "tok", [(s, s ^ flip) for s in range(parts)])

    turned = pl.pallas_call(
        functools.partial(turn_kernel, experts, cap),
        out_shape=pltpu.HBM((parts, depth + 16, rows), jnp.bfloat16),
        compiler_params=pltpu.CompilerParams(vmem_limit_bytes=16 * 2**20),
        name="turn",
    )(tokens, out_grads, routing.reshape(1, rows))

    held = {0: out_grads}
    if parts == 16:
        inward = [(s, s + 4) for s in range(4, 8)] + [(s, s - 4) for s in range(8, 12)]
        outward = [(s, s - 4) for s in range(4, 8)] + [(s, s + 4) for s in range(8, 12)]
        inner = (me // 4 == 1) | (me // 4 == 2)
        y_own = swap(out_grads, 2)
        near = swap(out_grads, 4)
        second = swap(out_grads, 8)
        y_own, near, second = lax.optimization_barrier((y_own, near, second))
        far = lax.ppermute(out_grads, "tok", inward)
        out = lax.ppermute(second, "tok", outward)
        y_near = swap(near, 2)
        (turned, far, out) = lax.optimization_barrier(
            (turned, far, out)
        )
        third = jnp.where(inner, far, out)
        y_second = swap(second, 2)
        held.update({4: near, 8: second, 12: third})
        held.update({2: y_own, 6: y_near, 10: y_second, 14: swap(third, 2)})
    else:
        flip = parts // 2
        while flip > 1:
            held.update({k ^ flip: swap(b, flip) for k, b in held.items()})
            flip //= 2
    held.update({k ^ 1: swap(b, 1) for k, b in held.items()})
    order = sorted(held)
    blocks = [held[k] for k in order]

    columns = lax.all_to_all(turned, "tok", split_axis=0, concat_axis=0, tiled=True)

    fisher, merged = pl.pallas_call(
        functools.partial(merge_kernel, experts, cap, tuple(order), width * hidden),
        grid=(hidden // TILE,),
        in_specs=[
            pl.BlockSpec(memory_space=pltpu.SMEM),
            pl.BlockSpec(memory_space=pltpu.VMEM),
            pl.BlockSpec((experts, depth, TILE), lambda f: (0, 0, f)),
        ]
        + [pl.BlockSpec((rows, TILE), lambda f: (0, f))] * len(blocks),
        out_specs=[
            pl.BlockSpec((experts, depth, TILE), lambda f: (0, 0, f)),
            pl.BlockSpec((depth, TILE), lambda f: (0, f)),
        ],
        out_shape=[
            jax.ShapeDtypeStruct((experts, depth, hidden), jnp.float32),
            jax.ShapeDtypeStruct((depth, hidden), jnp.bfloat16),
        ],
        scratch_shapes=[
            pltpu.VMEM((experts, depth, span), jnp.bfloat16),
            pltpu.VMEM((experts, depth, span), jnp.bfloat16),
            pltpu.VMEM((experts, span, TILE), jnp.bfloat16),
            pltpu.VMEM((experts, span, TILE), jnp.bfloat16),
            pltpu.VMEM((parts, experts * cap, rows), jnp.bfloat16),
            pltpu.VMEM((experts, TILE, (-(-TILE // cap) + 1) * rows), jnp.bfloat16),
            pltpu.VMEM((8, 128), jnp.float32),
        ],
        compiler_params=pltpu.CompilerParams(vmem_limit_bytes=52 * 2**20),
        name="merge",
    )(me.astype(jnp.int32)[None], columns, weights, *blocks)
    return (fisher, merged)


def solution(mesh):
    in_specs = (
        P(("layer", "tok"), None),
        P(("layer", "tok"), None),
        P(("layer", "tok"), None),
        P("layer", "tok", None),
    )
    out_specs = (P("layer", "tok", None), P(("layer", "tok"), None))
    body = functools.partial(local, mesh.shape["tok"])
    return jax.shard_map(body, mesh=mesh, in_specs=in_specs, out_specs=out_specs, check_vma=False)
```
